32 devices in a mesh: groups: 2 (over y), dp: 4 (over z), tensor: 4 (over x, core).
Axes of the slice: x: 2, y: 2, z: 4, core: 2. Of those that a mesh axis runs over, the one named last changes fastest.
Arguments:
- tokens: bfloat16 [4096, 8192], P(('groups', 'dp'), 'tensor'), parts along dimension 0, may hold values from -6 to 6
- norm_gain: float32 [8192], replicated, may hold values from 0.5 to 1.5
- w_inner: bfloat16 [8192, 8192], P('dp', 'tensor'), may hold values from -0.0625 to 0.0625
- w_groups: bfloat16 [8192, 2048], P('dp', 'tensor'), may hold values from -0.0625 to 0.0625
- w_keyval: bfloat16 [8192, 2048], P('dp', 'tensor'), may hold values from -0.0625 to 0.0625
- w_step: bfloat16 [8192, 128], P('dp', 'tensor'), may hold values from -0.0625 to 0.0625
- conv_inner: float32 [4, 8192], P(None, 'tensor'), may hold values from -3 to 3
- conv_groups: float32 [4, 2048], P(None, 'tensor'), may hold values from -3 to 3
- decay_rate: float32 [128], P('tensor'), may hold values from 0.01 to 1
- step_bias: float32 [128], P('tensor'), may hold values from -2 to 0.5
- page_counts: int32 [8, 8], P(('groups', 'dp')), parts along dimension 0, may hold values from 1 to 4, 16 in all within a row
- owners: int32 [64, 1], P(('groups', 'dp')), parts along dimension 0, may hold values from 0 to 3; in each aligned block of 8 rows (0 to 7, 8 to 15, ...) at most 2 rows name the same one
- page_owners: int32 [128, 1], P(('groups', 'dp')), parts along dimension 0, may hold values from 0 to 3; in each aligned block of 16 rows (0 to 15, 16 to 31, ...) at most 4 rows name the same one
Outputs:
- ssm_out: bfloat16 [4096, 8192], P(('groups', 'dp'), 'tensor'), parts along dimension 0
- handed_states: bfloat16 [64, 128, 64, 256], P(('groups', 'dp'), 'tensor'), parts along dimension 0
- handed_tails_inner: bfloat16 [64, 3, 8192], P(('groups', 'dp'), None, 'tensor'), parts along dimension 0
- handed_tails_groups: bfloat16 [64, 3, 2048], P(('groups', 'dp'), None, 'tensor'), parts along dimension 0
- handed_pages: bfloat16 [128, 32, 2048], P(('groups', 'dp'), None, 'tensor'), parts along dimension 0
The draws below stay inside these ranges and needn't reach their ends.
There are 2 independent parts, one for each index of `groups`. The reference program is written for one: setup_inputs(seed, part) draws one part's arguments, and reference() takes and returns one part's arrays. A program takes and returns all parts, laid end to end along the dimension named above; an argument that names none is the same for every part. Nothing has to cross between parts.
Inputs may be any that keep to these rules, and one draw needn't show every extreme that they name: `page_counts`: each request has at least one page; the pages of one index of dp sum to 16. `owners`: at most 2 requests of one index of dp go to one owner. `page_owners`: at most 4 pages of one index of dp go to one owner.
All inputs are finite; a program needn't handle non-finite values.
Results may differ from the reference program's by a relative error of at most 0.0085.
Values may be sent and summed in bfloat16 or wider, within the bound.
A program may use at most 192 MiB of HBM per device.

```python
import math
import jax
import jax.numpy as jnp
import numpy as np
from jax import lax

D = 8192
HEADS = 128
HEAD_DIM = 64
GROUPS = 4
STATE = 256
TOK_DEV = 512
PAGES = 16
REQ_DEV = 8
MOST_PAGES = 4
CAP = 2
PCAP = 4
INNER = 8192
GROUP_COLS = 2048
KV_COLS = 2048
PAGE = 32
TOKENS = 2048
REQS = 32
ALL_PAGES = 64
SLOTS = 32
PAGE_SLOTS = 64
N_DP = 4


def levels(key, extent, split, low, high):
    loudness = 1.0
    for axis_at, shards_of in split:
        heights = jax.random.uniform(jax.random.fold_in(jax.random.fold_in(key, 6), axis_at), (shards_of,), jnp.float32, low / len(split), high / len(split))
        loudness = loudness * jnp.repeat(jnp.exp(heights), extent[axis_at] // shards_of).reshape((-1,) + (1,) * (len(extent) - 1 - axis_at))
    return loudness


def profile(amount, total, most, slope):
    weights = [(1 << 20) // math.isqrt(rank ** slope) + 1 for rank in range(2, amount + 1)]
    rest, holding = total - most - (amount - 1), [1] * (amount - 1)
    while rest > 0:
        movable = [i for i in range(amount - 1) if holding[i] < most]
        whole, remaining = sum([weights[i] for i in movable]), rest
        for i in movable:
            extra = min(most - holding[i], max(1, remaining * weights[i] // whole), rest)
            holding[i] = holding[i] + extra
            rest = rest - extra
    return np.array([most] + holding)


def uneven(key, number_of, total, limit, skew):
    if number_of == 2:
        one = jax.random.randint(key, (), max(1, total - limit), min(limit, total - 1) + 1)
        return jnp.stack([one, total - one])
    lengths = jnp.asarray(profile(number_of, total, limit, skew), jnp.int32)
    pairs = (number_of - 1) // 2
    donor, taker = lengths[1:1 + 2 * pairs:2], lengths[2:2 + 2 * pairs:2]
    room = jnp.minimum(donor - 1, limit - taker)
    passed = jax.random.randint(jax.random.fold_in(key, 1), (pairs,), 0, 1 << 20) % (room + 1)
    lengths = lengths.at[1:1 + 2 * pairs:2].set(donor - passed).at[2:2 + 2 * pairs:2].set(taker + passed)
    return lengths[jax.random.permutation(jax.random.fold_in(key, 2), number_of)]


def shared_out(rng, own, number, rows, number_of, top, bound, slope):
    sequence = jax.random.permutation(rng, number_of)
    packed, usual = load_shares(number_of, rows * top, bound, slope, True), load_shares(number_of, rows * top, bound, slope, False)
    places = jnp.arange(number_of)

    def named(tallies, offset_by):
        used = int((tallies > 0).sum())
        fixed = max(1, used // 4)
        passed = fixed + (places - fixed + offset_by * (used - fixed)) % max(1, number_of - fixed)
        return jnp.zeros((number_of,), jnp.int32).at[sequence[jnp.where(places < fixed, places, passed)]].set(jnp.asarray(tallies, jnp.int32))

    tallies = jnp.where(number % 4 == 0, named(packed, number // 4), named(usual, number - number // 4 - 1))
    mixed = jax.random.permutation(jax.random.fold_in(own, 3), number_of)
    source_of, taker = mixed[0:number_of // 2 * 2:2], mixed[1:number_of // 2 * 2:2]
    margin = jnp.minimum(tallies[source_of] - 1, bound - tallies[taker]) // 2
    margin = jnp.where((source_of == sequence[0]) | (taker == sequence[0]) | (tallies[taker] == 0), 0, jnp.maximum(margin, 0))
    passed = jax.random.randint(jax.random.fold_in(own, 4), (number_of // 2,), 0, 1 << 20) % (margin + 1)
    tallies = tallies.at[source_of].add(-passed).at[taker].add(passed)
    members = jnp.searchsorted(jnp.cumsum(tallies), jnp.arange(rows * top), side="right").astype(jnp.int32)
    table = members.reshape(top, rows).T
    table = table[jax.random.permutation(jax.random.fold_in(own, 1), rows)]
    offset_by = jax.random.randint(jax.random.fold_in(own, 2), (rows, 1), 0, top)
    return jnp.take_along_axis(table, (jnp.arange(top)[None, :] + offset_by) % top, axis=1)


def load_shares(amount, total, limit, lean, full):
    portions = [(1 << 20) // math.isqrt(standing ** lean) + 1 for standing in range(1, amount + 1)]
    largest = limit if full else min(limit, max(-(-total // amount), total * portions[0] // sum(portions)))
    least = 1 if total - largest >= amount - 1 else 0
    given, surplus = [largest] + [least] * (amount - 1), total - largest - least * (amount - 1)
    while surplus > 0:
        free = [i for i in range(1, amount) if given[i] < largest] or [i for i in range(1, amount) if given[i] < limit]
        whole, remaining = sum([portions[i] for i in free]), surplus
        for i in free:
            more = min(limit - given[i], max(1, remaining * portions[i] // whole), surplus)
            given[i] = given[i] + more
            surplus = surplus - more
    return np.array(given)


def normal_values(key, extent, deviation, most, shards=(), kind=jnp.bfloat16):
    entries = jax.random.normal(key, extent, jnp.float32) * deviation
    if len(shards) > 0:
        entries = levels(key, extent, shards, -0.22, 0.18) * entries
    return jnp.clip(entries, min=-most, max=most).astype(kind)


def setup_inputs(seed: int = 0, part: int = 0) -> dict:
    streams_of = jax.random.split(jax.random.key(seed), 14)
    part_splits = jax.random.split(jax.random.fold_in(streams_of[13], part), 14)
    tokens = normal_values(part_splits[0], (TOKENS, D), 1.0, 6.0, ((0, 4), (1, 4)))
    norm_gain = jnp.clip(1.0 + 0.1 * jax.random.normal(streams_of[1], (D,), jnp.float32), 0.5, 1.5)
    w_inner = normal_values(streams_of[2], (D, INNER), D ** -0.5, 0.0625, ((0, 4), (1, 4)))
    w_groups = normal_values(streams_of[3], (D, GROUP_COLS), D ** -0.5, 0.0625, ((0, 4), (1, 4)))
    w_keyval = normal_values(streams_of[4], (D, KV_COLS), D ** -0.5, 0.0625, ((0, 4), (1, 4)))
    w_step = normal_values(streams_of[5], (D, HEADS), D ** -0.5, 0.0625, ((0, 4), (1, 4)))
    conv_inner = normal_values(streams_of[6], (4, INNER), 0.5, 3.0, ((1, 4),), jnp.float32)
    conv_groups = normal_values(streams_of[7], (4, GROUP_COLS), 0.5, 3.0, ((1, 4),), jnp.float32)
    decay_rate = jnp.clip(jnp.exp(math.log(1.0) - 4.6051702 * jax.random.uniform(streams_of[8], (HEADS,), jnp.float32) ** levels(streams_of[8], (HEADS,), ((0, 4),), -0.2, 0.2)), 0.01, 1.0)
    step_bias = jnp.clip(-2.0 + 2.5 * jax.random.uniform(streams_of[9], (HEADS,), jnp.float32) ** levels(streams_of[9], (HEADS,), ((0, 4),), -0.2, 0.2), -2.0, 0.5)
    page_counts = jax.vmap(lambda own: uneven(own, REQ_DEV, PAGES, MOST_PAGES, 1))(jax.random.split(part_splits[10], N_DP)).reshape((N_DP, REQ_DEV)).astype(jnp.int32)
    owners_keys = jax.random.split(jax.random.fold_in(part_splits[11], 1), REQS // REQ_DEV)
    owners_turns = jax.random.permutation(jax.random.fold_in(part_splits[11], 3), REQS // REQ_DEV)
    owners = jax.vmap(lambda own, number: shared_out(jax.random.fold_in(part_splits[11], 2), own, number, REQ_DEV, N_DP, 1, CAP, 2))(owners_keys, owners_turns).reshape((REQS, 1))
    page_owners_keys = jax.random.split(jax.random.fold_in(part_splits[12], 1), ALL_PAGES // PAGES)
    page_owners_turns = jax.random.permutation(jax.random.fold_in(part_splits[12], 3), ALL_PAGES // PAGES)
    page_owners = jax.vmap(lambda own, number: shared_out(jax.random.fold_in(part_splits[12], 2), own, number, PAGES, N_DP, 1, PCAP, 2))(page_owners_keys, page_owners_turns).reshape((ALL_PAGES, 1))
    return dict(tokens=tokens, norm_gain=norm_gain, w_inner=w_inner, w_groups=w_groups, w_keyval=w_keyval, w_step=w_step, conv_inner=conv_inner, conv_groups=conv_groups, decay_rate=decay_rate, step_bias=step_bias, page_counts=page_counts, owners=owners, page_owners=page_owners)


highest = lax.Precision.HIGHEST

def conv_silu(inputs, kernel, request_of):
    floats = inputs.astype(jnp.float32)
    total = kernel[3] * floats
    for offset in range(1, 4):
        moved = jnp.concatenate([jnp.zeros((offset, floats.shape[1]), jnp.float32), floats[:-offset]], 0)
        before = jnp.concatenate([jnp.full((offset,), -1, jnp.int32), request_of[:-offset]], 0)
        total = total + kernel[3 - offset] * jnp.where((before == request_of)[:, None], moved, jnp.float32(0.0))
    return jax.nn.silu(total).astype(jnp.bfloat16)

def request_layout(counts, rows_total, page_rows):
    ends = jnp.cumsum(counts).astype(jnp.int32)
    page_of = jnp.arange(rows_total, dtype=jnp.int32) // page_rows
    request_of = lax.optimization_barrier(jnp.sum((page_of[:, None] >= ends[None, :]).astype(jnp.int32), 1)).astype(jnp.int32)
    last_rows = (ends * page_rows - 1).astype(jnp.int32)
    return (request_of, last_rows)

def ssd_heads(values, widths, running, keys, queries, request_of, last_rows):
    scores = jnp.dot(queries, keys.T, preferred_element_type=jnp.float32)
    positions = jnp.arange(values.shape[0], dtype=jnp.int32)
    inside = (request_of[:, None] == request_of[None, :]) & (positions[None, :] <= positions[:, None])
    gaps = running.T[:, :, None] - running.T[:, None, :]
    decay = jnp.where(inside[None], jnp.exp(jnp.where(inside[None], gaps, jnp.float32(0.0))), jnp.float32(0.0))
    mixing = decay * scores[None]
    weighted = widths[:, :, None] * values
    outputs = jnp.einsum('hts,shd->thd', mixing, weighted, precision=highest)
    end_running = running[last_rows]
    requests = jnp.arange(last_rows.shape[0], dtype=jnp.int32)
    member = request_of[None, :] == requests[:, None]
    spans = end_running.T[:, :, None] - running.T[:, None, :]
    reach = jnp.where(member[None], jnp.exp(jnp.where(member[None], spans, jnp.float32(0.0))), jnp.float32(0.0))
    states = jnp.einsum('hrs,shd,sn->rhdn', reach, weighted, keys.astype(jnp.float32), precision=highest)
    return (outputs, states)

def slot_rows(targets, capacity):
    count = targets.shape[1]
    order = jnp.arange(count, dtype=jnp.int32)
    same = targets[:, None, :] == targets[:, :, None]
    earlier = order[None, None, :] < order[None, :, None]
    rank = lax.optimization_barrier(jnp.sum((same & earlier).astype(jnp.int32), 2)).astype(jnp.int32)
    source = jnp.arange(targets.shape[0], dtype=jnp.int32)[:, None]
    return (targets * (N_DP * capacity) + source * capacity + rank).reshape(-1).astype(jnp.int32)

def reference(tokens, norm_gain, w_inner, w_groups, w_keyval, w_step, conv_inner, conv_groups, decay_rate, step_bias, page_counts, owners, page_owners):
    floats = tokens.astype(jnp.float32)
    scale = lax.rsqrt(lax.optimization_barrier(jnp.mean(floats * floats, -1, keepdims=True)) + 1e-05)
    normed = (floats * scale * norm_gain).astype(jnp.bfloat16)
    inner_rows = jnp.dot(normed, w_inner, preferred_element_type=jnp.float32).astype(jnp.bfloat16)
    group_rows = jnp.dot(normed, w_groups, preferred_element_type=jnp.float32).astype(jnp.bfloat16)
    keyval = jnp.dot(normed, w_keyval, preferred_element_type=jnp.float32).astype(jnp.bfloat16)
    step_rows = jnp.dot(normed, w_step, preferred_element_type=jnp.float32).astype(jnp.bfloat16)
    per_group = HEADS // GROUPS

    def one_shard(pieces):
        inner_here, group_here, step_here, counts = pieces
        request_of, last_rows = request_layout(counts, TOK_DEV, PAGE)
        mixed = conv_silu(inner_here, conv_inner, request_of)
        grouped = conv_silu(group_here, conv_groups, request_of)
        widths = jax.nn.softplus(step_here.astype(jnp.float32) + step_bias)
        running = jnp.cumsum(-decay_rate * widths, 0)
        values = mixed.astype(jnp.float32).reshape(TOK_DEV, HEADS, HEAD_DIM)

        def one_group(group_id):
            first = group_id * per_group
            vals = lax.dynamic_slice_in_dim(values, first, per_group, 1)
            wide = lax.dynamic_slice_in_dim(widths, first, per_group, 1)
            runs = lax.dynamic_slice_in_dim(running, first, per_group, 1)
            keys = lax.dynamic_slice_in_dim(grouped, group_id * STATE, STATE, 1)
            queries = lax.dynamic_slice_in_dim(grouped, GROUPS * STATE + group_id * STATE, STATE, 1)
            return ssd_heads(vals, wide, runs, keys, queries, request_of, last_rows)
        outputs, states = lax.map(one_group, jnp.arange(GROUPS, dtype=jnp.int32))
        outputs = jnp.transpose(outputs, (1, 0, 2, 3)).reshape(TOK_DEV, INNER).astype(jnp.bfloat16)
        states = jnp.transpose(states, (1, 0, 2, 3, 4)).reshape(REQ_DEV, HEADS, HEAD_DIM, STATE).astype(jnp.bfloat16)
        tail_rows = last_rows[:, None] - 2 + jnp.arange(3, dtype=jnp.int32)[None, :]
        return (outputs, states, inner_here[tail_rows], group_here[tail_rows])
    pieces = (inner_rows.reshape(N_DP, TOK_DEV, INNER), group_rows.reshape(N_DP, TOK_DEV, GROUP_COLS), step_rows.reshape(N_DP, TOK_DEV, HEADS), page_counts)
    outputs, states, tails_inner, tails_groups = lax.map(one_shard, pieces)
    ssm_out = outputs.reshape(TOKENS, INNER)
    request_slots = slot_rows(owners.reshape(N_DP, REQ_DEV), CAP)
    handed_states = jnp.zeros((SLOTS, HEADS, HEAD_DIM, STATE), jnp.bfloat16).at[request_slots].set(states.reshape(REQS, HEADS, HEAD_DIM, STATE))
    handed_tails_inner = jnp.zeros((SLOTS, 3, INNER), jnp.bfloat16).at[request_slots].set(tails_inner.reshape(REQS, 3, INNER))
    handed_tails_groups = jnp.zeros((SLOTS, 3, GROUP_COLS), jnp.bfloat16).at[request_slots].set(tails_groups.reshape(REQS, 3, GROUP_COLS))
    page_slots = slot_rows(page_owners.reshape(N_DP, PAGES), PCAP)
    handed_pages = jnp.zeros((PAGE_SLOTS, PAGE, KV_COLS), jnp.bfloat16).at[page_slots].set(keyval.reshape(ALL_PAGES, PAGE, KV_COLS))
    return (ssm_out, handed_states, handed_tails_inner, handed_tails_groups, handed_pages)
```

```python
import jax
import jax.numpy as jnp
from jax import lax
from jax.sharding import PartitionSpec as P

HEADS = 128
HEAD_DIM = 64
GROUPS = 4
STATE = 256
CAP = 2
PCAP = 4
MOST_PAGES = 4

f32 = jnp.float32
bf16 = jnp.bfloat16


def conv_silu(inputs, kernel, request_of):
    floats = inputs.astype(f32)
    total = kernel[3] * floats
    for offset in range(1, 4):
        moved = jnp.concatenate(
            [jnp.zeros((offset, floats.shape[1]), f32), floats[:-offset]], 0
        )
        before = jnp.concatenate([jnp.full((offset,), -1, jnp.int32), request_of[:-offset]], 0)
        total = total + kernel[3 - offset] * jnp.where(
            (before == request_of)[:, None], moved, f32(0.0)
        )
    return jax.nn.silu(total).astype(bf16)


def request_layout(counts, rows_total, page_rows):
    ends = jnp.cumsum(counts)
    page_of = jnp.arange(rows_total, dtype=jnp.int32) // page_rows
    request_of = jnp.sum((page_of[:, None] >= ends[None, :]).astype(jnp.int32), 1)
    last_rows = ends * page_rows - 1
    return (request_of, last_rows, ends)


def ssd_outputs(values, widths, running, keys, queries, request_of):
    scores = jnp.dot(queries, keys.T, preferred_element_type=f32)
    positions = jnp.arange(values.shape[0], dtype=jnp.int32)
    inside = (request_of[:, None] == request_of[None, :]) & (
        positions[None, :] <= positions[:, None]
    )
    gaps = running.T[:, :, None] - running.T[:, None, :]
    decay = jnp.exp(jnp.where(inside[None], gaps, f32(-1e30)))
    mixing = (decay * scores[None]).astype(bf16)
    weighted = (widths[:, :, None] * values).astype(bf16)
    return jnp.einsum("hts,shd->thd", mixing, weighted, preferred_element_type=f32)


def ranks(targets):
    order = jnp.arange(targets.shape[0], dtype=jnp.int32)
    same = targets[None, :] == targets[:, None]
    return jnp.sum((same & (order[None, :] < order[:, None])).astype(jnp.int32), 1)


def slot_items(targets, owner_count, capacity):
    rank = ranks(targets)
    slot = targets * capacity + rank
    slots = jnp.arange(owner_count * capacity, dtype=jnp.int32)
    hit = slot[None, :] == slots[:, None]
    item = jnp.arange(targets.shape[0], dtype=jnp.int32)
    return jnp.sum(jnp.where(hit, item[None, :] + 1, 0), 1) - 1


def pick_rows(rows, table):
    picker = rows[:, None] == jnp.arange(table.shape[0], dtype=jnp.int32)[None, :]
    return jnp.dot(picker.astype(bf16), table, preferred_element_type=f32).astype(bf16)


def slot_of(source, features, count):
    half = count // 2
    swapped = (source % 2 + features) % 2
    return swapped * half + source // 2


def gather_features(scaled):
    dp_count = lax.axis_size("dp")
    tensor_count = lax.axis_size("tensor")
    rows, wide = scaled.shape
    me = lax.axis_index("dp")
    if dp_count == tensor_count and dp_count % 2 == 0:
        perm = []
        for source in range(dp_count):
            for features in range(dp_count):
                perm.append(
                    (
                        source * dp_count + features,
                        features * dp_count + slot_of(source, features, dp_count),
                    )
                )
        moved = lax.ppermute(scaled, ("dp", "tensor"), perm)
        gathered = lax.all_gather(moved, "tensor", axis=0)
        return [
            lax.dynamic_index_in_dim(gathered, slot_of(source, me, dp_count), 0, keepdims=False)
            for source in range(dp_count)
        ]
    full = lax.all_gather(scaled, "tensor", axis=1, tiled=True)
    split = full.reshape(rows, dp_count, -1).transpose(1, 0, 2)
    received = lax.all_to_all(split, "dp", split_axis=0, concat_axis=0, tiled=True)
    return [received[source] for source in range(dp_count)]


def exchange_sums(blocks, weights):
    partial = jnp.stack(
        [jnp.dot(b, weights, preferred_element_type=f32).astype(bf16) for b in blocks]
    )
    received = lax.all_to_all(partial, "dp", split_axis=0, concat_axis=0, tiled=True)
    return jnp.sum(received.astype(f32), 0)


def shards(
    tokens,
    norm_gain,
    w_inner,
    w_groups,
    w_keyval,
    w_step,
    conv_inner,
    conv_groups,
    decay_rate,
    step_bias,
    page_counts,
    owners,
    page_owners,
):
    rows_here, features_here = tokens.shape
    dp_count = lax.axis_size("dp")
    floats = tokens.astype(f32)
    gain = lax.dynamic_slice_in_dim(
        norm_gain, lax.axis_index("tensor") * features_here, features_here, 0
    )
    blocks = gather_features((floats * gain).astype(bf16))
    squares = lax.psum(jnp.sum(floats * floats, -1, keepdims=True), "tensor")
    features = features_here * lax.axis_size("tensor")
    scale = lax.rsqrt(squares / features + 1e-05)

    width_groups = w_groups.shape[1]
    heads_here = decay_rate.shape[0]
    small = jnp.concatenate([w_groups, w_step, w_keyval], 1)
    small_rows = (exchange_sums(blocks, small) * scale).astype(bf16)
    inner_rows = (exchange_sums(blocks, w_inner) * scale).astype(bf16)
    group_rows = small_rows[:, :width_groups]
    step_rows = small_rows[:, width_groups : width_groups + heads_here]
    keyval = small_rows[:, width_groups + heads_here :]

    page_total = page_owners.shape[0]
    page_rows = rows_here // page_total
    in_page = jnp.arange(page_rows, dtype=jnp.int32)
    request_of, last_rows, ends = request_layout(page_counts[0], rows_here, page_rows)

    page_items = slot_items(page_owners[:, 0], dp_count, PCAP)
    page_source = jnp.where(
        page_items[:, None] >= 0, page_items[:, None] * page_rows + in_page[None, :], -1
    )
    page_send = pick_rows(page_source.reshape(-1), keyval).reshape(
        dp_count, PCAP * page_rows, -1
    )

    grouped_local = conv_silu(group_rows, conv_groups, request_of)
    grouped = lax.all_gather(grouped_local, "tensor", axis=1, tiled=True)
    group_id = lax.axis_index("tensor") * heads_here // (HEADS // GROUPS)
    keys = lax.dynamic_slice_in_dim(grouped, group_id * STATE, STATE, 1)
    queries = lax.dynamic_slice_in_dim(grouped, GROUPS * STATE + group_id * STATE, STATE, 1)
    widths = jax.nn.softplus(step_rows.astype(f32) + step_bias)
    running = jnp.cumsum(-decay_rate * widths, 0)
    mixed = conv_silu(inner_rows, conv_inner, request_of)
    values = mixed.astype(f32).reshape(rows_here, heads_here, HEAD_DIM)

    end_running = running[last_rows]
    end_of = jnp.zeros_like(running)
    for r in range(page_counts.shape[1]):
        end_of = jnp.where((request_of == r)[:, None], end_running[r][None, :], end_of)
    reach = jnp.exp(end_of - running) * widths
    reached = (reach[:, :, None] * values).astype(bf16).reshape(rows_here, -1)

    slots = slot_items(owners[:, 0], dp_count, CAP)
    safe = jnp.maximum(slots, 0)
    counts = page_counts[0][safe]
    first = (ends[safe] - counts) * page_rows
    span = jnp.arange(MOST_PAGES * page_rows, dtype=jnp.int32)
    used = (slots[:, None] >= 0) & (span[None, :] < (counts * page_rows)[:, None])
    source = jnp.where(used, first[:, None] + span[None, :], -1).reshape(-1)
    value_send = pick_rows(source, reached).reshape(dp_count, CAP * span.shape[0], -1)
    key_send = pick_rows(source, keys).reshape(dp_count, CAP * span.shape[0], -1)
    tail = jnp.where(
        slots[:, None] >= 0,
        last_rows[safe][:, None] - 2 + jnp.arange(3, dtype=jnp.int32)[None, :],
        -1,
    ).reshape(-1)
    inner_send = pick_rows(tail, inner_rows).reshape(dp_count, CAP * 3, -1)
    group_send = pick_rows(tail, group_rows).reshape(dp_count, CAP * 3, -1)

    def swap(sent):
        return lax.all_to_all(sent, "dp", split_axis=0, concat_axis=0, tiled=True)

    page_received = swap(page_send)
    inner_received = swap(inner_send)
    group_received = swap(group_send)
    value_received = swap(value_send)
    key_received = swap(key_send)

    outputs = ssd_outputs(values, widths, running, keys, queries, request_of)
    ssm_out = outputs.reshape(rows_here, heads_here * HEAD_DIM).astype(bf16)

    slot_count = dp_count * CAP
    states = jnp.einsum(
        "osc,osn->ocn",
        value_received.reshape(slot_count, span.shape[0], -1),
        key_received.reshape(slot_count, span.shape[0], -1),
        preferred_element_type=f32,
    ).astype(bf16)
    return (
        ssm_out,
        states.reshape(slot_count, heads_here, HEAD_DIM, STATE),
        inner_received.reshape(slot_count, 3, -1),
        group_received.reshape(slot_count, 3, -1),
        page_received.reshape(dp_count * PCAP, page_rows, -1),
    )


def solution(mesh):
    in_specs = (
        P(("groups", "dp"), "tensor"),
        P(),
        P("dp", "tensor"),
        P("dp", "tensor"),
        P("dp", "tensor"),
        P("dp", "tensor"),
        P(None, "tensor"),
        P(None, "tensor"),
        P("tensor"),
        P("tensor"),
        P(("groups", "dp"), None),
        P(("groups", "dp"), None),
        P(("groups", "dp"), None),
    )
    out_specs = (
        P(("groups", "dp"), "tensor"),
        P(("groups", "dp"), "tensor", None, None),
        P(("groups", "dp"), None, "tensor"),
        P(("groups", "dp"), None, "tensor"),
        P(("groups", "dp"), None, "tensor"),
    )
    return jax.shard_map(shards, mesh=mesh, in_specs=in_specs, out_specs=out_specs, check_vma=False)
```

```python
import functools

import jax
import jax.numpy as jnp
from jax import lax
from jax.experimental import pallas as pl
from jax.experimental.pallas import tpu as pltpu
from jax.sharding import PartitionSpec as P

HEADS = 128
HEAD_DIM = 64
GROUPS = 4
STATE = 256
CAP = 2
PCAP = 4
MOST_PAGES = 4

f32 = jnp.float32
bf16 = jnp.bfloat16


def conv_silu(inputs, kernel, request_of):
    floats = inputs.astype(f32)
    total = kernel[3] * floats
    for offset in range(1, 4):
        moved = jnp.concatenate(
            [jnp.zeros((offset, floats.shape[1]), f32), floats[:-offset]], 0
        )
        before = jnp.concatenate([jnp.full((offset,), -1, jnp.int32), request_of[:-offset]], 0)
        total = total + kernel[3 - offset] * jnp.where(
            (before == request_of)[:, None], moved, f32(0.0)
        )
    return jax.nn.silu(total).astype(bf16)


def request_layout(counts, rows_total, page_rows):
    ends = jnp.cumsum(counts)
    page_of = jnp.arange(rows_total, dtype=jnp.int32) // page_rows
    request_of = jnp.sum((page_of[:, None] >= ends[None, :]).astype(jnp.int32), 1)
    last_rows = ends * page_rows - 1
    return (request_of, last_rows, ends)


def ssd_outputs(values, widths, running, keys, queries, request_of):
    scores = jnp.dot(queries, keys.T, preferred_element_type=f32)
    positions = jnp.arange(values.shape[0], dtype=jnp.int32)
    inside = (request_of[:, None] == request_of[None, :]) & (
        positions[None, :] <= positions[:, None]
    )
    gaps = running.T[:, :, None] - running.T[:, None, :]
    decay = jnp.exp(jnp.where(inside[None], gaps, f32(-1e30)))
    mixing = (decay * scores[None]).astype(bf16)
    weighted = (widths[:, :, None] * values).astype(bf16)
    return jnp.einsum("hts,shd->thd", mixing, weighted, preferred_element_type=f32)


def ranks(targets):
    order = jnp.arange(targets.shape[0], dtype=jnp.int32)
    same = targets[None, :] == targets[:, None]
    return jnp.sum((same & (order[None, :] < order[:, None])).astype(jnp.int32), 1)


def slot_items(targets, owner_count, capacity):
    rank = ranks(targets)
    slot = targets * capacity + rank
    slots = jnp.arange(owner_count * capacity, dtype=jnp.int32)
    hit = slot[None, :] == slots[:, None]
    item = jnp.arange(targets.shape[0], dtype=jnp.int32)
    return jnp.sum(jnp.where(hit, item[None, :] + 1, 0), 1) - 1


def pick_rows(rows, table):
    picker = rows[:, None] == jnp.arange(table.shape[0], dtype=jnp.int32)[None, :]
    return jnp.dot(picker.astype(bf16), table, preferred_element_type=f32).astype(bf16)


def slot_of(source, features, count):
    half = count // 2
    swapped = (source % 2 + features) % 2
    return swapped * half + source // 2


PIECES = 4
CHUNK = 640
MESH = pl.DeviceIdType.MESH
VMEM_LIMIT = 58 * 2**20


def share_kernel(count, x_ref, out_ref, send_sem, recv_sem):
    group = lax.axis_index("groups")
    dp = lax.axis_index("dp")
    ten = lax.axis_index("tensor")
    half = count // 2
    rows = x_ref.shape[0] // PIECES

    def source_at(slot):
        return lax.rem(slot, half) * 2 + lax.rem(slot // half + dp, 2)

    target = slot_of(dp, ten, count)
    mine = source_at(ten)
    sibling = ten + 1 - 2 * lax.rem(ten, 2)
    across = lax.rem(ten + half, count)
    beyond = lax.rem(sibling + half, count)
    stays = (ten == dp) & (target == ten)

    barrier = pltpu.get_barrier_semaphore()

    @pl.when(jnp.logical_not(stays))
    def _():
        pl.semaphore_signal(barrier, inc=1, device_id=(group, mine, dp), device_id_type=MESH)

    for peer in (sibling, across):
        pl.semaphore_signal(barrier, inc=1, device_id=(group, dp, peer), device_id_type=MESH)

    @pl.when(jnp.logical_not(stays))
    def _():
        pl.semaphore_wait(barrier, 3)

    @pl.when(stays)
    def _():
        pl.semaphore_wait(barrier, 2)

    def move(source, block, piece, kind, device):
        part = pl.ds(piece * rows, rows)
        return pltpu.make_async_remote_copy(
            src_ref=x_ref.at[part] if source is None else out_ref.at[source, part],
            dst_ref=out_ref.at[block, part],
            send_sem=send_sem.at[kind, piece],
            recv_sem=recv_sem.at[kind, piece],
            device_id=device,
            device_id_type=MESH,
        )

    def local(piece):
        part = pl.ds(piece * rows, rows)
        return pltpu.make_async_copy(x_ref.at[part], out_ref.at[dp, part], send_sem.at[0, piece])

    to_target = (group, ten, target)
    to_sibling = (group, dp, sibling)
    to_across = (group, dp, across)

    @pl.when(stays)
    def _():
        for piece in range(PIECES):
            local(piece).start()

    @pl.when(jnp.logical_not(stays))
    def _():
        for piece in range(PIECES):
            move(None, dp, piece, 0, to_target).start()

    for piece in range(PIECES):

        @pl.when(stays)
        def _():
            local(piece).wait()

        @pl.when(jnp.logical_not(stays))
        def _():
            move(None, mine, piece, 0, to_target).wait_recv()

        move(mine, mine, piece, 2, to_across).start()
        move(mine, mine, piece, 1, to_sibling).start()
    far = source_at(across)
    for piece in range(PIECES):
        move(far, far, piece, 2, to_across).wait_recv()
        move(far, far, piece, 3, to_sibling).start()
    near = source_at(sibling)
    last = source_at(beyond)
    for piece in range(PIECES):
        move(near, near, piece, 1, to_sibling).wait_recv()
        move(last, last, piece, 3, to_sibling).wait_recv()

    @pl.when(jnp.logical_not(stays))
    def _():
        for piece in range(PIECES):
            move(None, dp, piece, 0, to_target).wait_send()

    for piece in range(PIECES):
        move(mine, mine, piece, 2, to_across).wait_send()
        move(mine, mine, piece, 1, to_sibling).wait_send()
        move(far, far, piece, 3, to_sibling).wait_send()


def share_blocks(scaled):
    count = lax.axis_size("dp")
    return pl.pallas_call(
        functools.partial(share_kernel, count),
        out_shape=jax.ShapeDtypeStruct((count,) + scaled.shape, bf16),
        in_specs=[pl.BlockSpec(memory_space=pl.ANY)],
        out_specs=pl.BlockSpec(memory_space=pl.ANY),
        scratch_shapes=[
            pltpu.SemaphoreType.DMA((4, PIECES)),
            pltpu.SemaphoreType.DMA((4, PIECES)),
        ],
        compiler_params=pltpu.CompilerParams(collective_id=0, has_side_effects=True),
    )(scaled)


def line_kernel(
    count, widths, x_hbm, *refs
):
    weights = refs[: len(widths)]
    out_ref, x_ref, w_ref, held, part, load_sem, send_sem, recv_sem = refs[len(widths) :]
    group = lax.axis_index("groups")
    dp = lax.axis_index("dp")
    ten = lax.axis_index("tensor")
    chunks = w_ref.shape[1] // CHUNK

    loads = [pltpu.make_async_copy(x_hbm, x_ref, load_sem.at[0])]
    start = 0
    for index, width in enumerate(widths):
        loads.append(
            pltpu.make_async_copy(
                weights[index], w_ref.at[:, pl.ds(start, width)], load_sem.at[index + 1]
            )
        )
        start += width
    for load in loads:
        load.start()

    barrier = pltpu.get_barrier_semaphore()
    right = (group, dp + 1, ten)
    left = (group, dp - 1, ten)
    has_left = dp > 0
    has_right = dp < count - 1

    @pl.when(has_left)
    def _():
        pl.semaphore_signal(barrier, inc=1, device_id=left, device_id_type=MESH)

    @pl.when(has_right)
    def _():
        pl.semaphore_signal(barrier, inc=1, device_id=right, device_id_type=MESH)

    @pl.when(has_left & has_right)
    def _():
        pl.semaphore_wait(barrier, 2)

    @pl.when(jnp.logical_not(has_left & has_right))
    def _():
        pl.semaphore_wait(barrier, 1)

    for load in loads:
        load.wait()

    def move(slot, chunk, device):
        return pltpu.make_async_remote_copy(
            src_ref=held.at[slot, chunk],
            dst_ref=held.at[slot, chunk],
            send_sem=send_sem.at[slot, chunk],
            recv_sem=recv_sem.at[slot, chunk],
            device_id=device,
            device_id_type=MESH,
        )

    def project(block, chunk):
        columns = pl.ds(pl.multiple_of(chunk * CHUNK, 128), CHUNK)
        part[...] = jnp.dot(x_ref[block], w_ref[:, columns], preferred_element_type=f32)

    def step(block, slot, chunk, has_source, device):
        project(block, chunk)

        @pl.when(has_source)
        def _():
            move(slot, chunk, device).wait_recv()
            held[slot, chunk] = (part[...] + held[slot, chunk].astype(f32)).astype(bf16)

        @pl.when(jnp.logical_not(has_source))
        def _():
            held[slot, chunk] = part[...].astype(bf16)

        move(slot, chunk, device).start()

    @pl.loop(0, chunks)
    def _(chunk):
        @pl.loop(0, count - 1 - dp)
        def _(back):
            block = count - 1 - back
            step(block, block + 1, chunk, has_left, right)

        @pl.loop(0, dp)
        def _(block):
            step(block, block, chunk, has_right, left)

    @pl.loop(0, chunks)
    def _(chunk):
        columns = pl.ds(pl.multiple_of(chunk * CHUNK, 128), CHUNK)
        project(dp, chunk)

        @pl.when(has_left)
        def _():
            move(dp + 1, chunk, left).wait_recv()
            part[...] += held[dp + 1, chunk].astype(f32)

        @pl.when(has_right)
        def _():
            move(dp, chunk, right).wait_recv()
            part[...] += held[dp, chunk].astype(f32)

        out_ref[:, columns] = part[...]

    @pl.loop(0, chunks)
    def _(chunk):
        @pl.loop(0, count - 1 - dp)
        def _(back):
            move(count - back, chunk, right).wait_send()

        @pl.loop(0, dp)
        def _(block):
            move(block, chunk, left).wait_send()


def line_sums(blocks, weights):
    count, rows, depth = blocks.shape
    widths = [w.shape[1] for w in weights]
    total = sum(widths)
    chunks = total // CHUNK
    return pl.pallas_call(
        functools.partial(line_kernel, count, widths),
        out_shape=jax.ShapeDtypeStruct((rows, total), f32),
        in_specs=[pl.BlockSpec(memory_space=pl.ANY)] * (1 + len(weights)),
        out_specs=pl.BlockSpec(memory_space=pltpu.VMEM),
        scratch_shapes=[
            pltpu.VMEM((count, rows, depth), bf16),
            pltpu.VMEM((depth, total), bf16),
            pltpu.VMEM((count + 1, chunks, rows, CHUNK), bf16),
            pltpu.VMEM((rows, CHUNK), f32),
            pltpu.SemaphoreType.DMA((1 + len(weights),)),
            pltpu.SemaphoreType.DMA((count + 1, chunks)),
            pltpu.SemaphoreType.DMA((count + 1, chunks)),
        ],
        compiler_params=pltpu.CompilerParams(
            collective_id=1, has_side_effects=True, vmem_limit_bytes=VMEM_LIMIT
        ),
        cost_estimate=pl.CostEstimate(
            flops=2 * count * rows * depth * total,
            bytes_accessed=2 * (depth * total + count * rows * depth),
            transcendentals=0,
        ),
    )(blocks, *weights)


def pad_columns(weights, multiple):
    extra = -weights.shape[1] % multiple
    return jnp.pad(weights, ((0, 0), (0, extra)))


def gather_features(scaled):
    dp_count = lax.axis_size("dp")
    rows = scaled.shape[0]
    full = lax.all_gather(scaled, "tensor", axis=1, tiled=True)
    split = full.reshape(rows, dp_count, -1).transpose(1, 0, 2)
    received = lax.all_to_all(split, "dp", split_axis=0, concat_axis=0, tiled=True)
    return [received[source] for source in range(dp_count)]


def exchange_sums(blocks, weights):
    partial = jnp.stack(
        [jnp.dot(b, weights, preferred_element_type=f32).astype(bf16) for b in blocks]
    )
    received = lax.all_to_all(partial, "dp", split_axis=0, concat_axis=0, tiled=True)
    return jnp.sum(received.astype(f32), 0)


def shards(
    tokens,
    norm_gain,
    w_inner,
    w_groups,
    w_keyval,
    w_step,
    conv_inner,
    conv_groups,
    decay_rate,
    step_bias,
    page_counts,
    owners,
    page_owners,
):
    rows_here, features_here = tokens.shape
    dp_count = lax.axis_size("dp")
    floats = tokens.astype(f32)
    gain = lax.dynamic_slice_in_dim(
        norm_gain, lax.axis_index("tensor") * features_here, features_here, 0
    )
    scaled = (floats * gain).astype(bf16)
    squares = lax.psum(jnp.sum(floats * floats, -1, keepdims=True), "tensor")
    features = features_here * lax.axis_size("tensor")
    scale = lax.rsqrt(squares / features + 1e-05)

    width_groups = w_groups.shape[1]
    heads_here = decay_rate.shape[0]
    width_keyval = w_keyval.shape[1]
    pieces = [w_groups, w_keyval, pad_columns(w_step, 128), w_inner]
    total = sum(piece.shape[1] for piece in pieces)
    if dp_count == lax.axis_size("tensor") and dp_count == 4 and total % CHUNK == 0:
        sums = line_sums(share_blocks(scaled), pieces) * scale
    else:
        blocks = gather_features(scaled)
        sums = exchange_sums(blocks, jnp.concatenate(pieces, 1)) * scale
    group_rows = sums[:, :width_groups].astype(bf16)
    keyval = sums[:, width_groups : width_groups + width_keyval].astype(bf16)
    first_step = width_groups + width_keyval
    step_rows = sums[:, first_step : first_step + heads_here].astype(bf16)
    inner_rows = sums[:, total - w_inner.shape[1] :].astype(bf16)

    page_total = page_owners.shape[0]
    page_rows = rows_here // page_total
    in_page = jnp.arange(page_rows, dtype=jnp.int32)
    request_of, last_rows, ends = request_layout(page_counts[0], rows_here, page_rows)

    page_items = slot_items(page_owners[:, 0], dp_count, PCAP)
    page_source = jnp.where(
        page_items[:, None] >= 0, page_items[:, None] * page_rows + in_page[None, :], -1
    )
    page_send = pick_rows(page_source.reshape(-1), keyval).reshape(
        dp_count, PCAP * page_rows, -1
    )

    grouped_local = conv_silu(group_rows, conv_groups, request_of)
    grouped = lax.all_gather(grouped_local, "tensor", axis=1, tiled=True)
    group_id = lax.axis_index("tensor") * heads_here // (HEADS // GROUPS)
    keys = lax.dynamic_slice_in_dim(grouped, group_id * STATE, STATE, 1)
    queries = lax.dynamic_slice_in_dim(grouped, GROUPS * STATE + group_id * STATE, STATE, 1)
    widths = jax.nn.softplus(step_rows.astype(f32) + step_bias)
    running = jnp.cumsum(-decay_rate * widths, 0)
    mixed = conv_silu(inner_rows, conv_inner, request_of)
    values = mixed.astype(f32).reshape(rows_here, heads_here, HEAD_DIM)

    end_running = running[last_rows]
    end_of = jnp.zeros_like(running)
    for r in range(page_counts.shape[1]):
        end_of = jnp.where((request_of == r)[:, None], end_running[r][None, :], end_of)
    reach = jnp.exp(end_of - running) * widths
    reached = (reach[:, :, None] * values).astype(bf16).reshape(rows_here, -1)

    slots = slot_items(owners[:, 0], dp_count, CAP)
    safe = jnp.maximum(slots, 0)
    counts = page_counts[0][safe]
    first = (ends[safe] - counts) * page_rows
    span = jnp.arange(MOST_PAGES * page_rows, dtype=jnp.int32)
    used = (slots[:, None] >= 0) & (span[None, :] < (counts * page_rows)[:, None])
    source = jnp.where(used, first[:, None] + span[None, :], -1).reshape(-1)
    value_send = pick_rows(source, reached).reshape(dp_count, CAP * span.shape[0], -1)
    key_send = pick_rows(source, keys).reshape(dp_count, CAP * span.shape[0], -1)
    tail = jnp.where(
        slots[:, None] >= 0,
        last_rows[safe][:, None] - 2 + jnp.arange(3, dtype=jnp.int32)[None, :],
        -1,
    ).reshape(-1)
    inner_send = pick_rows(tail, inner_rows).reshape(dp_count, CAP * 3, -1)
    group_send = pick_rows(tail, group_rows).reshape(dp_count, CAP * 3, -1)

    def swap(sent):
        return lax.all_to_all(sent, "dp", split_axis=0, concat_axis=0, tiled=True)

    page_received = swap(page_send)
    inner_received = swap(inner_send)
    group_received = swap(group_send)
    value_received = swap(value_send)
    key_received = swap(key_send)

    outputs = ssd_outputs(values, widths, running, keys, queries, request_of)
    ssm_out = outputs.reshape(rows_here, heads_here * HEAD_DIM).astype(bf16)

    slot_count = dp_count * CAP
    states = jnp.einsum(
        "osc,osn->ocn",
        value_received.reshape(slot_count, span.shape[0], -1),
        key_received.reshape(slot_count, span.shape[0], -1),
        preferred_element_type=f32,
    ).astype(bf16)
    return (
        ssm_out,
        states.reshape(slot_count, heads_here, HEAD_DIM, STATE),
        inner_received.reshape(slot_count, 3, -1),
        group_received.reshape(slot_count, 3, -1),
        page_received.reshape(dp_count * PCAP, page_rows, -1),
    )


def solution(mesh):
    in_specs = (
        P(("groups", "dp"), "tensor"),
        P(),
        P("dp", "tensor"),
        P("dp", "tensor"),
        P("dp", "tensor"),
        P("dp", "tensor"),
        P(None, "tensor"),
        P(None, "tensor"),
        P("tensor"),
        P("tensor"),
        P(("groups", "dp"), None),
        P(("groups", "dp"), None),
        P(("groups", "dp"), None),
    )
    out_specs = (
        P(("groups", "dp"), "tensor"),
        P(("groups", "dp"), "tensor", None, None),
        P(("groups", "dp"), None, "tensor"),
        P(("groups", "dp"), None, "tensor"),
        P(("groups", "dp"), None, "tensor"),
    )
    return jax.shard_map(shards, mesh=mesh, in_specs=in_specs, out_specs=out_specs, check_vma=False)
```

```python
import functools

import jax
import jax.numpy as jnp
from jax import lax
from jax.experimental import pallas as pl
from jax.experimental.pallas import tpu as pltpu
from jax.sharding import PartitionSpec as P

HEADS = 128
HEAD_DIM = 64
GROUPS = 4
STATE = 256
CAP = 2
PCAP = 4
MOST_PAGES = 4

f32 = jnp.float32
bf16 = jnp.bfloat16


def conv_silu(inputs, kernel, request_of):
    floats = inputs.astype(f32)
    total = kernel[3] * floats
    for offset in range(1, 4):
        moved = jnp.concatenate(
            [jnp.zeros((offset, floats.shape[1]), f32), floats[:-offset]], 0
        )
        before = jnp.concatenate([jnp.full((offset,), -1, jnp.int32), request_of[:-offset]], 0)
        total = total + kernel[3 - offset] * jnp.where(
            (before == request_of)[:, None], moved, f32(0.0)
        )
    return jax.nn.silu(total).astype(bf16)


def request_layout(counts, rows_total, page_rows):
    ends = jnp.cumsum(counts)
    page_of = jnp.arange(rows_total, dtype=jnp.int32) // page_rows
    request_of = jnp.sum((page_of[:, None] >= ends[None, :]).astype(jnp.int32), 1)
    last_rows = ends * page_rows - 1
    return (request_of, last_rows, ends)


def ssd_outputs(weighted, running, keys, queries, request_of):
    scores = jnp.dot(queries, keys.T, preferred_element_type=f32)
    positions = jnp.arange(weighted.shape[0], dtype=jnp.int32)
    inside = (request_of[:, None] == request_of[None, :]) & (
        positions[None, :] <= positions[:, None]
    )
    gaps = running.T[:, :, None] - running.T[:, None, :]
    decay = jnp.exp(jnp.where(inside[None], gaps, f32(-1e30)))
    mixing = (decay * scores[None]).astype(bf16)
    return jnp.einsum("hts,shd->thd", mixing, weighted, preferred_element_type=f32)


def spread(per_head):
    heads = per_head.shape[1]
    channel = jnp.arange(heads * HEAD_DIM, dtype=jnp.int32) // HEAD_DIM
    table = (channel[None, :] == jnp.arange(heads, dtype=jnp.int32)[:, None]).astype(f32)
    return jnp.dot(per_head, table, precision=lax.Precision.HIGHEST)


def ranks(targets):
    order = jnp.arange(targets.shape[0], dtype=jnp.int32)
    same = targets[None, :] == targets[:, None]
    return jnp.sum((same & (order[None, :] < order[:, None])).astype(jnp.int32), 1)


def slot_items(targets, owner_count, capacity):
    rank = ranks(targets)
    slot = targets * capacity + rank
    slots = jnp.arange(owner_count * capacity, dtype=jnp.int32)
    hit = slot[None, :] == slots[:, None]
    item = jnp.arange(targets.shape[0], dtype=jnp.int32)
    return jnp.sum(jnp.where(hit, item[None, :] + 1, 0), 1) - 1


def pick_rows(rows, table):
    picker = rows[:, None] == jnp.arange(table.shape[0], dtype=jnp.int32)[None, :]
    return jnp.dot(picker.astype(bf16), table, preferred_element_type=f32).astype(bf16)


def slot_of(source, features, count):
    half = count // 2
    swapped = (source % 2 + features) % 2
    return swapped * half + source // 2


PIECES = 8
CHUNK = 640
MESH = pl.DeviceIdType.MESH
VMEM_LIMIT = 58 * 2**20


def share_kernel(count, x_ref, out_ref, send_sem, recv_sem):
    group = lax.axis_index("groups")
    dp = lax.axis_index("dp")
    ten = lax.axis_index("tensor")
    half = count // 2
    rows = x_ref.shape[0] // PIECES

    def source_at(slot):
        return lax.rem(slot, half) * 2 + lax.rem(slot // half + dp, 2)

    target = slot_of(dp, ten, count)
    mine = source_at(ten)
    sibling = ten + 1 - 2 * lax.rem(ten, 2)
    across = lax.rem(ten + half, count)
    beyond = lax.rem(sibling + half, count)
    stays = (ten == dp) & (target == ten)

    barrier = pltpu.get_barrier_semaphore()

    @pl.when(jnp.logical_not(stays))
    def _():
        pl.semaphore_signal(barrier, inc=1, device_id=(group, mine, dp), device_id_type=MESH)

    for peer in (sibling, across):
        pl.semaphore_signal(barrier, inc=1, device_id=(group, dp, peer), device_id_type=MESH)

    @pl.when(jnp.logical_not(stays))
    def _():
        pl.semaphore_wait(barrier, 3)

    @pl.when(stays)
    def _():
        pl.semaphore_wait(barrier, 2)

    def move(source, block, piece, kind, device):
        part = pl.ds(piece * rows, rows)
        return pltpu.make_async_remote_copy(
            src_ref=x_ref.at[part] if source is None else out_ref.at[source, part],
            dst_ref=out_ref.at[block, part],
            send_sem=send_sem.at[kind, piece],
            recv_sem=recv_sem.at[kind, piece],
            device_id=device,
            device_id_type=MESH,
        )

    def local(piece):
        part = pl.ds(piece * rows, rows)
        return pltpu.make_async_copy(x_ref.at[part], out_ref.at[dp, part], send_sem.at[0, piece])

    to_target = (group, ten, target)
    to_sibling = (group, dp, sibling)
    to_across = (group, dp, across)

    @pl.when(stays)
    def _():
        for piece in range(PIECES):
            local(piece).start()

    @pl.when(jnp.logical_not(stays))
    def _():
        for piece in range(PIECES):
            move(None, dp, piece, 0, to_target).start()

    for piece in range(PIECES):

        @pl.when(stays)
        def _():
            local(piece).wait()

        @pl.when(jnp.logical_not(stays))
        def _():
            move(None, mine, piece, 0, to_target).wait_recv()

        move(mine, mine, piece, 2, to_across).start()
        move(mine, mine, piece, 1, to_sibling).start()
    far = source_at(across)
    for piece in range(PIECES):
        move(far, far, piece, 2, to_across).wait_recv()
        move(far, far, piece, 3, to_sibling).start()
    near = source_at(sibling)
    last = source_at(beyond)
    for piece in range(PIECES):
        move(near, near, piece, 1, to_sibling).wait_recv()
        move(last, last, piece, 3, to_sibling).wait_recv()

    @pl.when(jnp.logical_not(stays))
    def _():
        for piece in range(PIECES):
            move(None, dp, piece, 0, to_target).wait_send()

    for piece in range(PIECES):
        move(mine, mine, piece, 2, to_across).wait_send()
        move(mine, mine, piece, 1, to_sibling).wait_send()
        move(far, far, piece, 3, to_sibling).wait_send()


def share_blocks(scaled):
    count = lax.axis_size("dp")
    return pl.pallas_call(
        functools.partial(share_kernel, count),
        out_shape=jax.ShapeDtypeStruct((count,) + scaled.shape, bf16),
        in_specs=[pl.BlockSpec(memory_space=pl.ANY)],
        out_specs=pl.BlockSpec(memory_space=pl.ANY),
        scratch_shapes=[
            pltpu.SemaphoreType.DMA((4, PIECES)),
            pltpu.SemaphoreType.DMA((4, PIECES)),
        ],
        compiler_params=pltpu.CompilerParams(collective_id=0, has_side_effects=True),
    )(scaled)


def line_kernel(
    count, widths, x_hbm, *refs
):
    weights = refs[: len(widths)]
    out_ref, x_ref, w_ref, held, part, load_sem, send_sem, recv_sem = refs[len(widths) :]
    group = lax.axis_index("groups")
    dp = lax.axis_index("dp")
    ten = lax.axis_index("tensor")
    chunks = w_ref.shape[1] // CHUNK

    loads = [pltpu.make_async_copy(x_hbm, x_ref, load_sem.at[0])]
    start = 0
    for index, width in enumerate(widths):
        loads.append(
            pltpu.make_async_copy(
                weights[index], w_ref.at[:, pl.ds(start, width)], load_sem.at[index + 1]
            )
        )
        start += width
    for load in loads:
        load.start()

    barrier = pltpu.get_barrier_semaphore()
    right = (group, dp + 1, ten)
    left = (group, dp - 1, ten)
    has_left = dp > 0
    has_right = dp < count - 1

    @pl.when(has_left)
    def _():
        pl.semaphore_signal(barrier, inc=1, device_id=left, device_id_type=MESH)

    @pl.when(has_right)
    def _():
        pl.semaphore_signal(barrier, inc=1, device_id=right, device_id_type=MESH)

    @pl.when(has_left & has_right)
    def _():
        pl.semaphore_wait(barrier, 2)

    @pl.when(jnp.logical_not(has_left & has_right))
    def _():
        pl.semaphore_wait(barrier, 1)

    for load in loads:
        load.wait()

    def move(slot, chunk, device):
        return pltpu.make_async_remote_copy(
            src_ref=held.at[slot, chunk],
            dst_ref=held.at[slot, chunk],
            send_sem=send_sem.at[slot, chunk],
            recv_sem=recv_sem.at[slot, chunk],
            device_id=device,
            device_id_type=MESH,
        )

    def project(block, chunk):
        columns = pl.ds(pl.multiple_of(chunk * CHUNK, 128), CHUNK)
        part[...] = jnp.dot(x_ref[block], w_ref[:, columns], preferred_element_type=f32)

    def step(block, slot, chunk, has_source, device):
        project(block, chunk)

        @pl.when(has_source)
        def _():
            move(slot, chunk, device).wait_recv()
            held[slot, chunk] = (part[...] + held[slot, chunk].astype(f32)).astype(bf16)

        @pl.when(jnp.logical_not(has_source))
        def _():
            held[slot, chunk] = part[...].astype(bf16)

        move(slot, chunk, device).start()

    @pl.loop(0, chunks)
    def _(chunk):
        @pl.loop(0, count - 1 - dp)
        def _(back):
            block = count - 1 - back
            step(block, block + 1, chunk, has_left, right)

        @pl.loop(0, dp)
        def _(block):
            step(block, block, chunk, has_right, left)

    @pl.loop(0, chunks)
    def _(chunk):
        columns = pl.ds(pl.multiple_of(chunk * CHUNK, 128), CHUNK)
        project(dp, chunk)

        @pl.when(has_left)
        def _():
            move(dp + 1, chunk, left).wait_recv()
            part[...] += held[dp + 1, chunk].astype(f32)

        @pl.when(has_right)
        def _():
            move(dp, chunk, right).wait_recv()
            part[...] += held[dp, chunk].astype(f32)

        out_ref[:, columns] = part[...]

    @pl.loop(0, chunks)
    def _(chunk):
        @pl.loop(0, count - 1 - dp)
        def _(back):
            move(count - back, chunk, right).wait_send()

        @pl.loop(0, dp)
        def _(block):
            move(block, chunk, left).wait_send()


def line_sums(blocks, weights):
    count, rows, depth = blocks.shape
    widths = [w.shape[1] for w in weights]
    total = sum(widths)
    chunks = total // CHUNK
    return pl.pallas_call(
        functools.partial(line_kernel, count, widths),
        out_shape=jax.ShapeDtypeStruct((rows, total), f32),
        in_specs=[pl.BlockSpec(memory_space=pl.ANY)] * (1 + len(weights)),
        out_specs=pl.BlockSpec(memory_space=pltpu.VMEM),
        scratch_shapes=[
            pltpu.VMEM((count, rows, depth), bf16),
            pltpu.VMEM((depth, total), bf16),
            pltpu.VMEM((count + 1, chunks, rows, CHUNK), bf16),
            pltpu.VMEM((rows, CHUNK), f32),
            pltpu.SemaphoreType.DMA((1 + len(weights),)),
            pltpu.SemaphoreType.DMA((count + 1, chunks)),
            pltpu.SemaphoreType.DMA((count + 1, chunks)),
        ],
        compiler_params=pltpu.CompilerParams(
            collective_id=1, has_side_effects=True, vmem_limit_bytes=VMEM_LIMIT
        ),
        cost_estimate=pl.CostEstimate(
            flops=2 * count * rows * depth * total,
            bytes_accessed=2 * (depth * total + count * rows * depth),
            transcendentals=0,
        ),
    )(blocks, *weights)


def pad_columns(weights, multiple):
    extra = -weights.shape[1] % multiple
    return jnp.pad(weights, ((0, 0), (0, extra)))


def gather_features(scaled):
    dp_count = lax.axis_size("dp")
    rows = scaled.shape[0]
    full = lax.all_gather(scaled, "tensor", axis=1, tiled=True)
    split = full.reshape(rows, dp_count, -1).transpose(1, 0, 2)
    received = lax.all_to_all(split, "dp", split_axis=0, concat_axis=0, tiled=True)
    return [received[source] for source in range(dp_count)]


def exchange_sums(blocks, weights):
    partial = jnp.stack(
        [jnp.dot(b, weights, preferred_element_type=f32).astype(bf16) for b in blocks]
    )
    received = lax.all_to_all(partial, "dp", split_axis=0, concat_axis=0, tiled=True)
    return jnp.sum(received.astype(f32), 0)


def shards(
    tokens,
    norm_gain,
    w_inner,
    w_groups,
    w_keyval,
    w_step,
    conv_inner,
    conv_groups,
    decay_rate,
    step_bias,
    page_counts,
    owners,
    page_owners,
):
    rows_here, features_here = tokens.shape
    dp_count = lax.axis_size("dp")
    floats = tokens.astype(f32)
    gain = lax.dynamic_slice_in_dim(
        norm_gain, lax.axis_index("tensor") * features_here, features_here, 0
    )
    scaled = (floats * gain).astype(bf16)
    squares = lax.psum(jnp.sum(floats * floats, -1, keepdims=True), "tensor")
    features = features_here * lax.axis_size("tensor")
    scale = lax.rsqrt(squares / features + 1e-05)

    width_groups = w_groups.shape[1]
    heads_here = decay_rate.shape[0]
    width_keyval = w_keyval.shape[1]
    pieces = [w_groups, w_keyval, pad_columns(w_step, 128), w_inner]
    total = sum(piece.shape[1] for piece in pieces)
    if dp_count == lax.axis_size("tensor") and dp_count == 4 and total % CHUNK == 0:
        sums = line_sums(share_blocks(scaled), pieces) * scale
    else:
        blocks = gather_features(scaled)
        sums = exchange_sums(blocks, jnp.concatenate(pieces, 1)) * scale
    group_rows = sums[:, :width_groups].astype(bf16)
    keyval = sums[:, width_groups : width_groups + width_keyval].astype(bf16)
    first_step = width_groups + width_keyval
    step_rows = sums[:, first_step : first_step + heads_here].astype(bf16)
    inner_rows = sums[:, total - w_inner.shape[1] :].astype(bf16)

    page_total = page_owners.shape[0]
    page_rows = rows_here // page_total
    in_page = jnp.arange(page_rows, dtype=jnp.int32)
    request_of, last_rows, ends = request_layout(page_counts[0], rows_here, page_rows)

    grouped_local = conv_silu(group_rows, conv_groups, request_of)
    grouped = lax.all_gather(grouped_local, "tensor", axis=1, tiled=True)
    group_id = lax.axis_index("tensor") * heads_here // (HEADS // GROUPS)
    keys = lax.dynamic_slice_in_dim(grouped, group_id * STATE, STATE, 1)
    queries = lax.dynamic_slice_in_dim(grouped, GROUPS * STATE + group_id * STATE, STATE, 1)
    widths = jax.nn.softplus(step_rows.astype(f32) + step_bias)
    running = jnp.cumsum(-decay_rate * widths, 0)
    mixed = conv_silu(inner_rows, conv_inner, request_of)

    end_running = running[last_rows]
    end_of = jnp.zeros_like(running)
    for r in range(page_counts.shape[1]):
        end_of = jnp.where((request_of == r)[:, None], end_running[r][None, :], end_of)
    reach = jnp.exp(end_of - running) * widths
    reached = (spread(reach) * mixed.astype(f32)).astype(bf16)

    slots = slot_items(owners[:, 0], dp_count, CAP)
    safe = jnp.maximum(slots, 0)
    counts = page_counts[0][safe]
    first = (ends[safe] - counts) * page_rows
    span = jnp.arange(MOST_PAGES * page_rows, dtype=jnp.int32)
    used = (slots[:, None] >= 0) & (span[None, :] < (counts * page_rows)[:, None])
    source = jnp.where(used, first[:, None] + span[None, :], -1).reshape(-1)
    tail = jnp.where(
        slots[:, None] >= 0,
        last_rows[safe][:, None] - 2 + jnp.arange(3, dtype=jnp.int32)[None, :],
        -1,
    ).reshape(-1)
    page_items = slot_items(page_owners[:, 0], dp_count, PCAP)
    page_source = jnp.where(
        page_items[:, None] >= 0, page_items[:, None] * page_rows + in_page[None, :], -1
    ).reshape(-1)

    def picked(rows, table):
        return pick_rows(rows, table).reshape(dp_count, -1, table.shape[1])

    def halves(items):
        half = items.shape[2] // 2
        return jnp.concatenate([items[:, :, :half], items[:, :, half:]], 1)

    def whole(items):
        half = items.shape[1] // 2
        return jnp.concatenate([items[:, :half], items[:, half:]], 2)

    def swap(sent):
        return lax.all_to_all(sent, "dp", split_axis=0, concat_axis=0, tiled=True)

    wide = w_inner.shape[1]
    value_rows = CAP * span.shape[0]
    tail_rows = CAP * 3
    tails = picked(tail, jnp.concatenate([inner_rows, group_rows], 1))
    inner_tail = jnp.pad(tails[:, :, :wide], ((0, 0), (0, 16 - tail_rows), (0, 0)))
    group_tail = jnp.pad(halves(tails[:, :, wide:]), ((0, 0), (0, 16 - 2 * tail_rows), (0, 0)))
    main_send = jnp.concatenate(
        [
            jnp.concatenate([picked(source, reached), halves(picked(page_source, keyval))], 2),
            jnp.concatenate([inner_tail, group_tail], 2),
        ],
        1,
    )
    main = swap(main_send)
    keys_after, _ = lax.optimization_barrier((keys, main_send))
    key_received = swap(picked(source, keys_after))

    weighted = (spread(widths) * mixed.astype(f32)).astype(bf16)
    weighted = weighted.reshape(rows_here, heads_here, HEAD_DIM)
    outputs = ssd_outputs(weighted, running, keys, queries, request_of)
    ssm_out = outputs.reshape(rows_here, heads_here * HEAD_DIM).astype(bf16)

    value_received = main[:, :value_rows, :wide]
    page_received = whole(main[:, :value_rows, wide:])
    inner_received = main[:, value_rows : value_rows + tail_rows, :wide]
    group_received = whole(main[:, value_rows : value_rows + 2 * tail_rows, wide:])

    slot_count = dp_count * CAP
    states = jnp.einsum(
        "osc,osn->ocn",
        value_received.reshape(slot_count, span.shape[0], -1),
        key_received.reshape(slot_count, span.shape[0], -1),
        preferred_element_type=f32,
    ).astype(bf16)
    return (
        ssm_out,
        states.reshape(slot_count, heads_here, HEAD_DIM, STATE),
        inner_received.reshape(slot_count, 3, -1),
        group_received.reshape(slot_count, 3, -1),
        page_received.reshape(dp_count * PCAP, page_rows, -1),
    )


def solution(mesh):
    in_specs = (
        P(("groups", "dp"), "tensor"),
        P(),
        P("dp", "tensor"),
        P("dp", "tensor"),
        P("dp", "tensor"),
        P("dp", "tensor"),
        P(None, "tensor"),
        P(None, "tensor"),
        P("tensor"),
        P("tensor"),
        P(("groups", "dp"), None),
        P(("groups", "dp"), None),
        P(("groups", "dp"), None),
    )
    out_specs = (
        P(("groups", "dp"), "tensor"),
        P(("groups", "dp"), "tensor", None, None),
        P(("groups", "dp"), None, "tensor"),
        P(("groups", "dp"), None, "tensor"),
        P(("groups", "dp"), None, "tensor"),
    )
    return jax.shard_map(shards, mesh=mesh, in_specs=in_specs, out_specs=out_specs, check_vma=False)
```

```python
import functools

import jax
import jax.numpy as jnp
from jax import lax
from jax.experimental import pallas as pl
from jax.experimental.pallas import tpu as pltpu
from jax.sharding import PartitionSpec as P

HEADS = 128
HEAD_DIM = 64
GROUPS = 4
STATE = 256
CAP = 2
PCAP = 4
MOST_PAGES = 4

f32 = jnp.float32
bf16 = jnp.bfloat16


def conv_silu(inputs, kernel, request_of):
    floats = inputs.astype(f32)
    total = kernel[3] * floats
    for offset in range(1, 4):
        moved = jnp.concatenate(
            [jnp.zeros((offset, floats.shape[1]), f32), floats[:-offset]], 0
        )
        before = jnp.concatenate([jnp.full((offset,), -1, jnp.int32), request_of[:-offset]], 0)
        total = total + kernel[3 - offset] * jnp.where(
            (before == request_of)[:, None], moved, f32(0.0)
        )
    return jax.nn.silu(total).astype(bf16)


def request_layout(counts, rows_total, page_rows):
    ends = jnp.cumsum(counts)
    page_of = jnp.arange(rows_total, dtype=jnp.int32) // page_rows
    request_of = jnp.sum((page_of[:, None] >= ends[None, :]).astype(jnp.int32), 1)
    last_rows = ends * page_rows - 1
    return (request_of, last_rows, ends)


def ssd_outputs(weighted, running, keys, queries, request_of):
    scores = jnp.dot(queries, keys.T, preferred_element_type=f32)
    positions = jnp.arange(weighted.shape[0], dtype=jnp.int32)
    inside = (request_of[:, None] == request_of[None, :]) & (
        positions[None, :] <= positions[:, None]
    )
    gaps = running.T[:, :, None] - running.T[:, None, :]
    decay = jnp.exp(jnp.where(inside[None], gaps, f32(-1e30)))
    mixing = (decay * scores[None]).astype(bf16)
    return jnp.einsum("hts,shd->thd", mixing, weighted, preferred_element_type=f32)


def spread(per_head):
    heads = per_head.shape[1]
    channel = jnp.arange(heads * HEAD_DIM, dtype=jnp.int32) // HEAD_DIM
    table = (channel[None, :] == jnp.arange(heads, dtype=jnp.int32)[:, None]).astype(f32)
    return jnp.dot(per_head, table, precision=lax.Precision.HIGHEST)


def ranks(targets):
    order = jnp.arange(targets.shape[0], dtype=jnp.int32)
    same = targets[None, :] == targets[:, None]
    return jnp.sum((same & (order[None, :] < order[:, None])).astype(jnp.int32), 1)


def slot_items(targets, owner_count, capacity):
    rank = ranks(targets)
    slot = targets * capacity + rank
    slots = jnp.arange(owner_count * capacity, dtype=jnp.int32)
    hit = slot[None, :] == slots[:, None]
    item = jnp.arange(targets.shape[0], dtype=jnp.int32)
    return jnp.sum(jnp.where(hit, item[None, :] + 1, 0), 1) - 1


def pick_rows(rows, table):
    picker = rows[:, None] == jnp.arange(table.shape[0], dtype=jnp.int32)[None, :]
    return jnp.dot(picker.astype(bf16), table, preferred_element_type=f32).astype(bf16)


def slot_of(source, features, count):
    half = count // 2
    swapped = (source % 2 + features) % 2
    return swapped * half + source // 2


PIECES = 8
CHUNK = 640
MESH = pl.DeviceIdType.MESH
VMEM_LIMIT = 58 * 2**20


def share_kernel(count, x_ref, out_ref, send_sem, recv_sem):
    group = lax.axis_index("groups")
    dp = lax.axis_index("dp")
    ten = lax.axis_index("tensor")
    half = count // 2
    rows = x_ref.shape[0] // PIECES

    def source_at(slot):
        return lax.rem(slot, half) * 2 + lax.rem(slot // half + dp, 2)

    target = slot_of(dp, ten, count)
    mine = source_at(ten)
    sibling = ten + 1 - 2 * lax.rem(ten, 2)
    across = lax.rem(ten + half, count)
    beyond = lax.rem(sibling + half, count)
    stays = (ten == dp) & (target == ten)

    barrier = pltpu.get_barrier_semaphore()

    @pl.when(jnp.logical_not(stays))
    def _():
        pl.semaphore_signal(barrier, inc=1, device_id=(group, mine, dp), device_id_type=MESH)

    for peer in (sibling, across):
        pl.semaphore_signal(barrier, inc=1, device_id=(group, dp, peer), device_id_type=MESH)

    @pl.when(jnp.logical_not(stays))
    def _():
        pl.semaphore_wait(barrier, 3)

    @pl.when(stays)
    def _():
        pl.semaphore_wait(barrier, 2)

    def move(source, block, piece, kind, device):
        part = pl.ds(piece * rows, rows)
        return pltpu.make_async_remote_copy(
            src_ref=x_ref.at[part] if source is None else out_ref.at[source, part],
            dst_ref=out_ref.at[block, part],
            send_sem=send_sem.at[kind, piece],
            recv_sem=recv_sem.at[kind, piece],
            device_id=device,
            device_id_type=MESH,
        )

    def local(piece):
        part = pl.ds(piece * rows, rows)
        return pltpu.make_async_copy(x_ref.at[part], out_ref.at[dp, part], send_sem.at[0, piece])

    to_target = (group, ten, target)
    to_sibling = (group, dp, sibling)
    to_across = (group, dp, across)

    @pl.when(stays)
    def _():
        for piece in range(PIECES):
            local(piece).start()

    @pl.when(jnp.logical_not(stays))
    def _():
        for piece in range(PIECES):
            move(None, dp, piece, 0, to_target).start()

    for piece in range(PIECES):

        @pl.when(stays)
        def _():
            local(piece).wait()

        @pl.when(jnp.logical_not(stays))
        def _():
            move(None, mine, piece, 0, to_target).wait_recv()

        move(mine, mine, piece, 2, to_across).start()
        move(mine, mine, piece, 1, to_sibling).start()
    far = source_at(across)
    for piece in range(PIECES):
        move(far, far, piece, 2, to_across).wait_recv()
        move(far, far, piece, 3, to_sibling).start()
    near = source_at(sibling)
    last = source_at(beyond)
    for piece in range(PIECES):
        move(near, near, piece, 1, to_sibling).wait_recv()
        move(last, last, piece, 3, to_sibling).wait_recv()

    @pl.when(jnp.logical_not(stays))
    def _():
        for piece in range(PIECES):
            move(None, dp, piece, 0, to_target).wait_send()

    for piece in range(PIECES):
        move(mine, mine, piece, 2, to_across).wait_send()
        move(mine, mine, piece, 1, to_sibling).wait_send()
        move(far, far, piece, 3, to_sibling).wait_send()


def share_blocks(scaled):
    count = lax.axis_size("dp")
    return pl.pallas_call(
        functools.partial(share_kernel, count),
        out_shape=jax.ShapeDtypeStruct((count,) + scaled.shape, bf16),
        in_specs=[pl.BlockSpec(memory_space=pl.ANY)],
        out_specs=pl.BlockSpec(memory_space=pl.ANY),
        scratch_shapes=[
            pltpu.SemaphoreType.DMA((4, PIECES)),
            pltpu.SemaphoreType.DMA((4, PIECES)),
        ],
        compiler_params=pltpu.CompilerParams(collective_id=0, has_side_effects=True),
    )(scaled)


def line_kernel(
    count, widths, x_hbm, *refs
):
    weights = refs[: len(widths)]
    out_ref, x_ref, w_ref, held, part, load_sem, send_sem, recv_sem = refs[len(widths) :]
    group = lax.axis_index("groups")
    dp = lax.axis_index("dp")
    ten = lax.axis_index("tensor")
    chunks = w_ref.shape[1] // CHUNK

    loads = [pltpu.make_async_copy(x_hbm, x_ref, load_sem.at[0])]
    start = 0
    for index, width in enumerate(widths):
        loads.append(
            pltpu.make_async_copy(
                weights[index], w_ref.at[:, pl.ds(start, width)], load_sem.at[index + 1]
            )
        )
        start += width
    for load in loads:
        load.start()

    barrier = pltpu.get_barrier_semaphore()
    right = (group, dp + 1, ten)
    left = (group, dp - 1, ten)
    has_left = dp > 0
    has_right = dp < count - 1

    @pl.when(has_left)
    def _():
        pl.semaphore_signal(barrier, inc=1, device_id=left, device_id_type=MESH)

    @pl.when(has_right)
    def _():
        pl.semaphore_signal(barrier, inc=1, device_id=right, device_id_type=MESH)

    @pl.when(has_left & has_right)
    def _():
        pl.semaphore_wait(barrier, 2)

    @pl.when(jnp.logical_not(has_left & has_right))
    def _():
        pl.semaphore_wait(barrier, 1)

    for load in loads:
        load.wait()

    def move(slot, chunk, device):
        return pltpu.make_async_remote_copy(
            src_ref=held.at[slot, chunk],
            dst_ref=held.at[slot, chunk],
            send_sem=send_sem.at[slot, chunk],
            recv_sem=recv_sem.at[slot, chunk],
            device_id=device,
            device_id_type=MESH,
        )

    def project(block, chunk):
        columns = pl.ds(pl.multiple_of(chunk * CHUNK, 128), CHUNK)
        part[...] = jnp.dot(x_ref[block], w_ref[:, columns], preferred_element_type=f32)

    def step(block, slot, chunk, has_source, device):
        project(block, chunk)

        @pl.when(has_source)
        def _():
            move(slot, chunk, device).wait_recv()
            held[slot, chunk] = (part[...] + held[slot, chunk].astype(f32)).astype(bf16)

        @pl.when(jnp.logical_not(has_source))
        def _():
            held[slot, chunk] = part[...].astype(bf16)

        move(slot, chunk, device).start()

    @pl.loop(0, chunks)
    def _(chunk):
        @pl.loop(0, count - 1 - dp)
        def _(back):
            block = count - 1 - back
            step(block, block + 1, chunk, has_left, right)

        @pl.loop(0, dp)
        def _(block):
            step(block, block, chunk, has_right, left)

    @pl.loop(0, chunks)
    def _(chunk):
        columns = pl.ds(pl.multiple_of(chunk * CHUNK, 128), CHUNK)
        project(dp, chunk)

        @pl.when(has_left)
        def _():
            move(dp + 1, chunk, left).wait_recv()
            part[...] += held[dp + 1, chunk].astype(f32)

        @pl.when(has_right)
        def _():
            move(dp, chunk, right).wait_recv()
            part[...] += held[dp, chunk].astype(f32)

        out_ref[:, columns] = part[...]

    @pl.loop(0, chunks)
    def _(chunk):
        @pl.loop(0, count - 1 - dp)
        def _(back):
            move(count - back, chunk, right).wait_send()

        @pl.loop(0, dp)
        def _(block):
            move(block, chunk, left).wait_send()


def line_sums(blocks, weights):
    count, rows, depth = blocks.shape
    widths = [w.shape[1] for w in weights]
    total = sum(widths)
    chunks = total // CHUNK
    return pl.pallas_call(
        functools.partial(line_kernel, count, widths),
        out_shape=jax.ShapeDtypeStruct((rows, total), f32),
        in_specs=[pl.BlockSpec(memory_space=pl.ANY)] * (1 + len(weights)),
        out_specs=pl.BlockSpec(memory_space=pltpu.VMEM),
        scratch_shapes=[
            pltpu.VMEM((count, rows, depth), bf16),
            pltpu.VMEM((depth, total), bf16),
            pltpu.VMEM((count + 1, chunks, rows, CHUNK), bf16),
            pltpu.VMEM((rows, CHUNK), f32),
            pltpu.SemaphoreType.DMA((1 + len(weights),)),
            pltpu.SemaphoreType.DMA((count + 1, chunks)),
            pltpu.SemaphoreType.DMA((count + 1, chunks)),
        ],
        compiler_params=pltpu.CompilerParams(
            collective_id=1, has_side_effects=True, vmem_limit_bytes=VMEM_LIMIT
        ),
        cost_estimate=pl.CostEstimate(
            flops=2 * count * rows * depth * total,
            bytes_accessed=2 * (depth * total + count * rows * depth),
            transcendentals=0,
        ),
    )(blocks, *weights)


def pad_columns(weights, multiple):
    extra = -weights.shape[1] % multiple
    return jnp.pad(weights, ((0, 0), (0, extra)))


def gather_features(scaled):
    dp_count = lax.axis_size("dp")
    rows = scaled.shape[0]
    full = lax.all_gather(scaled, "tensor", axis=1, tiled=True)
    split = full.reshape(rows, dp_count, -1).transpose(1, 0, 2)
    received = lax.all_to_all(split, "dp", split_axis=0, concat_axis=0, tiled=True)
    return [received[source] for source in range(dp_count)]


def exchange_sums(blocks, weights):
    partial = jnp.stack(
        [jnp.dot(b, weights, preferred_element_type=f32).astype(bf16) for b in blocks]
    )
    received = lax.all_to_all(partial, "dp", split_axis=0, concat_axis=0, tiled=True)
    return jnp.sum(received.astype(f32), 0)


def shards(
    tokens,
    norm_gain,
    w_inner,
    w_groups,
    w_keyval,
    w_step,
    conv_inner,
    conv_groups,
    decay_rate,
    step_bias,
    page_counts,
    owners,
    page_owners,
):
    rows_here, features_here = tokens.shape
    dp_count = lax.axis_size("dp")
    floats = tokens.astype(f32)
    gain = lax.dynamic_slice_in_dim(
        norm_gain, lax.axis_index("tensor") * features_here, features_here, 0
    )
    scaled = (floats * gain).astype(bf16)
    squares = lax.psum(jnp.sum(floats * floats, -1, keepdims=True), "tensor")
    features = features_here * lax.axis_size("tensor")
    scale = lax.rsqrt(squares / features + 1e-05)

    width_groups = w_groups.shape[1]
    heads_here = decay_rate.shape[0]
    width_keyval = w_keyval.shape[1]
    pieces = [w_groups, w_keyval, pad_columns(w_step, 128), w_inner]
    total = sum(piece.shape[1] for piece in pieces)
    if dp_count == lax.axis_size("tensor") and dp_count == 4 and total % CHUNK == 0:
        sums = line_sums(share_blocks(scaled), pieces) * scale
    else:
        blocks = gather_features(scaled)
        sums = exchange_sums(blocks, jnp.concatenate(pieces, 1)) * scale
    group_rows = sums[:, :width_groups].astype(bf16)
    keyval = sums[:, width_groups : width_groups + width_keyval].astype(bf16)
    first_step = width_groups + width_keyval
    step_rows = sums[:, first_step : first_step + heads_here].astype(bf16)
    inner_rows = sums[:, total - w_inner.shape[1] :].astype(bf16)

    page_total = page_owners.shape[0]
    page_rows = rows_here // page_total
    in_page = jnp.arange(page_rows, dtype=jnp.int32)
    request_of, last_rows, ends = request_layout(page_counts[0], rows_here, page_rows)

    grouped_local = conv_silu(group_rows, conv_groups, request_of)
    grouped = lax.all_gather(grouped_local, "tensor", axis=1, tiled=True)
    group_id = lax.axis_index("tensor") * heads_here // (HEADS // GROUPS)
    keys = lax.dynamic_slice_in_dim(grouped, group_id * STATE, STATE, 1)
    queries = lax.dynamic_slice_in_dim(grouped, GROUPS * STATE + group_id * STATE, STATE, 1)
    widths = jax.nn.softplus(step_rows.astype(f32) + step_bias)
    running = jnp.cumsum(-decay_rate * widths, 0)
    mixed = conv_silu(inner_rows, conv_inner, request_of)

    end_running = running[last_rows]
    end_of = jnp.zeros_like(running)
    for r in range(page_counts.shape[1]):
        end_of = jnp.where((request_of == r)[:, None], end_running[r][None, :], end_of)
    reach = jnp.exp(end_of - running) * widths
    reached = (spread(reach) * mixed.astype(f32)).astype(bf16)

    slots = slot_items(owners[:, 0], dp_count, CAP)
    safe = jnp.maximum(slots, 0)
    counts = page_counts[0][safe]
    first = (ends[safe] - counts) * page_rows
    span = jnp.arange(MOST_PAGES * page_rows, dtype=jnp.int32)
    used = (slots[:, None] >= 0) & (span[None, :] < (counts * page_rows)[:, None])
    source = jnp.where(used, first[:, None] + span[None, :], -1).reshape(-1)
    tail = jnp.where(
        slots[:, None] >= 0,
        last_rows[safe][:, None] - 2 + jnp.arange(3, dtype=jnp.int32)[None, :],
        -1,
    ).reshape(-1)
    page_items = slot_items(page_owners[:, 0], dp_count, PCAP)
    page_source = jnp.where(
        page_items[:, None] >= 0, page_items[:, None] * page_rows + in_page[None, :], -1
    ).reshape(-1)

    def picked(rows, table):
        return pick_rows(rows, table).reshape(dp_count, -1, table.shape[1])

    def halves(items):
        half = items.shape[2] // 2
        return jnp.concatenate([items[:, :, :half], items[:, :, half:]], 1)

    def whole(items):
        half = items.shape[1] // 2
        return jnp.concatenate([items[:, :half], items[:, half:]], 2)

    def swap(sent):
        return lax.all_to_all(sent, "dp", split_axis=0, concat_axis=0, tiled=True)

    wide = w_inner.shape[1]
    value_rows = CAP * span.shape[0]
    tail_rows = CAP * 3
    tails = picked(tail, jnp.concatenate([inner_rows, group_rows], 1))
    inner_tail = jnp.pad(tails[:, :, :wide], ((0, 0), (0, 16 - tail_rows), (0, 0)))
    group_tail = jnp.pad(halves(tails[:, :, wide:]), ((0, 0), (0, 16 - 2 * tail_rows), (0, 0)))
    main_send = jnp.concatenate(
        [
            jnp.concatenate([picked(source, reached), halves(picked(page_source, keyval))], 2),
            jnp.concatenate([inner_tail, group_tail], 2),
        ],
        1,
    )
    main = swap(main_send)

    weighted = (spread(widths) * mixed.astype(f32)).astype(bf16)
    weighted = weighted.reshape(rows_here, heads_here, HEAD_DIM)
    outputs = ssd_outputs(weighted, running, keys, queries, request_of)
    ssm_out = outputs.reshape(rows_here, heads_here * HEAD_DIM).astype(bf16)

    keys_after, ssm_out = lax.optimization_barrier((keys, ssm_out))
    key_received = swap(picked(source, keys_after))

    value_received = main[:, :value_rows, :wide]
    page_received = whole(main[:, :value_rows, wide:])
    inner_received = main[:, value_rows : value_rows + tail_rows, :wide]
    group_received = whole(main[:, value_rows : value_rows + 2 * tail_rows, wide:])

    slot_count = dp_count * CAP
    states = jnp.einsum(
        "osc,osn->ocn",
        value_received.reshape(slot_count, span.shape[0], -1),
        key_received.reshape(slot_count, span.shape[0], -1),
        preferred_element_type=f32,
    ).astype(bf16)
    return (
        ssm_out,
        states.reshape(slot_count, heads_here, HEAD_DIM, STATE),
        inner_received.reshape(slot_count, 3, -1),
        group_received.reshape(slot_count, 3, -1),
        page_received.reshape(dp_count * PCAP, page_rows, -1),
    )


def solution(mesh):
    in_specs = (
        P(("groups", "dp"), "tensor"),
        P(),
        P("dp", "tensor"),
        P("dp", "tensor"),
        P("dp", "tensor"),
        P("dp", "tensor"),
        P(None, "tensor"),
        P(None, "tensor"),
        P("tensor"),
        P("tensor"),
        P(("groups", "dp"), None),
        P(("groups", "dp"), None),
        P(("groups", "dp"), None),
    )
    out_specs = (
        P(("groups", "dp"), "tensor"),
        P(("groups", "dp"), "tensor", None, None),
        P(("groups", "dp"), None, "tensor"),
        P(("groups", "dp"), None, "tensor"),
        P(("groups", "dp"), None, "tensor"),
    )
    return jax.shard_map(shards, mesh=mesh, in_specs=in_specs, out_specs=out_specs, check_vma=False)
```
